32 devices in a mesh: group: 2 (over x), segment: 8 (over z, y), tensor: 2 (over core).
Axes of the slice: x: 2, y: 2, z: 4, core: 2. Of those that a mesh axis runs over, the one named last changes fastest.
Arguments:
- stream_in: bfloat16 [64, 8192], P('group', 'tensor'), parts along dimension 0, may hold values from -6 to 6
- cache_k: bfloat16 [8, 512, 16, 1024], P('segment', 'group', None, 'tensor'), parts along dimension 1, may hold values from -7 to 7
- cache_v: bfloat16 [8, 512, 16, 1024], P('segment', 'group', None, 'tensor'), parts along dimension 1, may hold values from -6 to 6
- new_k: bfloat16 [8, 64, 1024], P('segment', 'group', 'tensor'), parts along dimension 1, may hold values from -6 to 6
- new_v: bfloat16 [8, 64, 1024], P('segment', 'group', 'tensor'), parts along dimension 1, may hold values from -6 to 6
- q_gain: bfloat16 [8, 8192], P('segment', 'tensor'), may hold values from 0.25 to 1.75
- page_table: int32 [64, 8], P('group'), parts along dimension 0, may hold values from 0 to 255, as said below
- lengths: int32 [64], P('group'), parts along dimension 0, may hold values from 1 to 128, as said below
Outputs:
- streams: bfloat16 [8, 64, 8192], P('segment', 'group', 'tensor'), parts along dimension 1
- replica_k: bfloat16 [8, 64, 16, 1024], P('segment', 'group', None, 'tensor'), parts along dimension 1
- replica_v: bfloat16 [8, 64, 16, 1024], P('segment', 'group', None, 'tensor'), parts along dimension 1
The draws below stay inside these ranges and needn't reach their ends.
There are 2 independent parts, one for each index of `group`. The reference program is written for one: setup_inputs(seed, part) draws one part's arguments, and reference() takes and returns one part's arrays. A program takes and returns all parts, laid end to end along the dimension named above; an argument that names none is the same for every part. Nothing has to cross between parts.
Inputs may be any that keep to these rules, and one draw needn't show every extreme that they name: `page_table`: each part's page table holds every pool page exactly once. `lengths`: about half of the rows end on a page boundary; some row holds the full 8 * 16 tokens.
All inputs are finite; a program needn't handle non-finite values.
Results may differ from the reference program's by a relative error of at most 0.012.
Values may be sent and summed in bfloat16 or wider, within the bound.
A program may use at most 64 MiB of HBM per device.

```python
import jax
import jax.numpy as jnp
from jax import lax

D = 8192
KV_HEADS = 8
HEAD_DIM = 128
PAGE = 16
MAXP = 8
ROWS = 32
POOL = 256
SEGMENTS = 8


def draw_page_table(key, part):
    key = jax.random.fold_in(key, 11)
    order = jax.random.permutation(key, POOL).astype(jnp.int32)
    return order.reshape(ROWS, MAXP)


def draw_lengths(key, part):
    key = jax.random.fold_in(key, 22)
    key_full, key_pages, key_tail, key_pick = jax.random.split(key, 4)
    full_pages = jax.random.randint(key_full, (ROWS,), 1, MAXP + 1) * PAGE
    partial_value = jax.random.randint(key_pages, (ROWS,), 0, MAXP) * PAGE + jax.random.randint(key_tail, (ROWS,), 1, PAGE)
    pick = jax.random.randint(key_pick, (ROWS,), 0, 2)
    result = jnp.where(pick == 1, full_pages, partial_value).astype(jnp.int32)
    return result.at[0].set(MAXP * PAGE)


def draw_cache_k(key, part):
    key = jax.random.fold_in(key, 33)
    key_value = jax.random.fold_in(key, 1)
    shape = (SEGMENTS, POOL, PAGE, KV_HEADS * HEAD_DIM)
    values = jnp.clip(jax.random.normal(key_value, shape, jnp.float32), -4.0, 4.0)
    return values.astype(jnp.bfloat16)


def level_of(rng, extent, cuts, least, largest):
    level = 1.0
    for dim, blocks in cuts:
        steps = jax.random.uniform(jax.random.fold_in(jax.random.fold_in(rng, 6), dim), (blocks,), jnp.float32, least / len(cuts), largest / len(cuts))
        level = level * jnp.repeat(jnp.exp(steps), extent[dim] // blocks).reshape((-1,) + (1,) * (len(extent) - 1 - dim))
    return level


def scatter_about(key, extent, scale, most, shards=(), kind=jnp.bfloat16):
    values = scale * jax.random.normal(key, extent, jnp.float32)
    if shards:
        values = values * level_of(key, extent, shards, -0.22, 0.18)
    return jnp.clip(values, -most, most).astype(kind)


def setup_inputs(seed: int = 0, part: int = 0) -> dict:
    streams_of = jax.random.split(jax.random.key(seed), 9)
    part_splits = jax.random.split(jax.random.fold_in(streams_of[8], part), 9)
    return {
        "stream_in": scatter_about(part_splits[0], (ROWS, D), 1.0, 6.0, ((1, 2),)),
        "cache_k": draw_cache_k(jax.random.fold_in(jax.random.fold_in(streams_of[8], part), 71), part),
        "cache_v": scatter_about(part_splits[2], (SEGMENTS, POOL, PAGE, KV_HEADS * HEAD_DIM), 1.0, 6.0, ((0, 8), (3, 2))),
        "new_k": scatter_about(part_splits[3], (SEGMENTS, ROWS, KV_HEADS * HEAD_DIM), 1.0, 6.0, ((0, 8), (2, 2))),
        "new_v": scatter_about(part_splits[4], (SEGMENTS, ROWS, KV_HEADS * HEAD_DIM), 1.0, 6.0, ((0, 8), (2, 2))),
        "q_gain": jnp.clip(1.0 + 0.15 * jax.random.normal(streams_of[5], (SEGMENTS, D), jnp.float32), 0.25, 1.75).astype(jnp.bfloat16),
        "page_table": draw_page_table(jax.random.fold_in(jax.random.fold_in(streams_of[8], part), 71), part),
        "lengths": draw_lengths(jax.random.fold_in(jax.random.fold_in(streams_of[8], part), 71), part),
    }


EPSILON = 1e-06

def section_attention(current, keys_pool, values_pool, fresh_key, fresh_value, gain, page_table, lengths):
    rows = current.shape[0]
    width = current.shape[1]
    heads_here = width // HEAD_DIM
    kv_here = keys_pool.shape[-1] // HEAD_DIM
    group_size = heads_here // kv_here
    context = page_table.shape[1] * PAGE
    widened = current.astype(jnp.float32).reshape(rows, heads_here, HEAD_DIM)
    mean_square = lax.optimization_barrier(jnp.mean(widened * widened, axis=-1, keepdims=True))
    query = (widened * lax.rsqrt(mean_square + EPSILON) * gain.astype(jnp.float32).reshape(heads_here, HEAD_DIM)).astype(jnp.bfloat16)
    query = query.reshape(rows, kv_here, group_size, HEAD_DIM).astype(jnp.float32)
    keys = keys_pool[page_table].reshape(rows, context, kv_here, HEAD_DIM).astype(jnp.float32)
    values = values_pool[page_table].reshape(rows, context, kv_here, HEAD_DIM).astype(jnp.float32)
    fresh_k = fresh_key.reshape(rows, kv_here, HEAD_DIM).astype(jnp.float32)
    fresh_v = fresh_value.reshape(rows, kv_here, HEAD_DIM).astype(jnp.float32)
    score_scale = HEAD_DIM ** (-0.5)
    scores = jnp.einsum('rkgd,rtkd->rkgt', query, keys) * score_scale
    own_score = jnp.einsum('rkgd,rkd->rkg', query, fresh_k) * score_scale
    visible = (jnp.arange(context)[None, :] < lengths[:, None])[:, None, None, :]
    scores = jnp.where(visible, scores, -1e+30)
    highest = jnp.maximum(lax.optimization_barrier(jnp.max(scores, axis=-1)), own_score)
    weights = jnp.where(visible, jnp.exp(scores - highest[..., None]), 0.0)
    own_weight = jnp.exp(own_score - highest)
    denominator = lax.optimization_barrier(jnp.sum(weights, axis=-1)) + own_weight
    weights = (weights / denominator[..., None]).astype(jnp.bfloat16).astype(jnp.float32)
    own_weight = (own_weight / denominator).astype(jnp.bfloat16).astype(jnp.float32)
    mixed = jnp.einsum('rkgt,rtkd->rkgd', weights, values) + own_weight[..., None] * fresh_v[:, :, None, :]
    return (current.astype(jnp.float32) + mixed.reshape(rows, width)).astype(jnp.bfloat16)

def reference(stream_in, cache_k, cache_v, new_k, new_v, q_gain, page_table, lengths):

    def one_section(stream, pieces):
        keys_pool, values_pool, fresh_key, fresh_value, gain = pieces
        result = section_attention(stream, keys_pool, values_pool, fresh_key, fresh_value, gain, page_table, lengths)
        return (result, result)
    final_stream, streams = lax.scan(one_section, stream_in, (cache_k, cache_v, new_k, new_v, q_gain))
    finished = lengths % PAGE == 0
    last_page = jnp.maximum(lengths // PAGE - 1, 0).astype(jnp.int32)
    page_ids = jnp.take_along_axis(page_table, last_page[:, None], axis=1)[:, 0]
    keep = finished[None, :, None, None]
    picked_k = cache_k[:, page_ids]
    picked_v = cache_v[:, page_ids]
    picked_k = jnp.where(keep, picked_k, jnp.zeros_like(picked_k))
    picked_v = jnp.where(keep, picked_v, jnp.zeros_like(picked_v))
    return (streams, jnp.roll(picked_k, 1, axis=0), jnp.roll(picked_v, 1, axis=0))
```

```python
import functools

import jax
import jax.numpy as jnp
from jax import lax
from jax.experimental import pallas as pl
from jax.experimental.pallas import tpu as pltpu
from jax.sharding import PartitionSpec as P

HEAD_DIM = 128
PAGE = 16
EPSILON = 1e-06
SCALE = HEAD_DIM ** (-0.5)
CHUNK = 8


def relay_kernel(
    sections,
    x_ref, k_ref, v_ref, nk_ref, nv_ref, gain_ref, table_ref, length_ref,
    out_ref, rk_ref, rv_ref,
    k_pool, v_pool, x_in, stage_k, stage_v, pool_sem, recv_sem, send_sem, rep_send, rep_recv,
):
    rows, heads, _ = x_in.shape
    kv = k_pool.shape[2] // HEAD_DIM
    share = heads // kv
    pages = table_ref.shape[1]
    context = pages * PAGE
    chunks = rows // CHUNK
    me = lax.axis_index("segment")
    right = lax.rem(me + 1, sections)
    left = lax.rem(me + sections - 1, sections)

    load_k = pltpu.make_async_copy(k_ref, k_pool, pool_sem.at[0])
    load_v = pltpu.make_async_copy(v_ref, v_pool, pool_sem.at[1])
    load_k.start()
    load_v.start()

    barrier = pltpu.get_barrier_semaphore()
    for neighbour in (left, right):
        pl.semaphore_signal(
            barrier, inc=1, device_id={"segment": neighbour}, device_id_type=pl.DeviceIdType.MESH
        )
    pl.semaphore_wait(barrier, 2)

    def rows_of(c):
        return pl.ds(c * CHUNK, CHUNK)

    @pl.when(me == 0)
    def _():
        for c in range(chunks):
            pltpu.make_async_copy(
                x_ref.at[rows_of(c)], x_in.at[rows_of(c)], recv_sem.at[c]
            ).start()

    def send_of(c):
        return pltpu.make_async_remote_copy(
            src_ref=out_ref.at[rows_of(c)],
            dst_ref=x_in.at[rows_of(c)],
            send_sem=send_sem.at[c],
            recv_sem=recv_sem.at[c],
            device_id={"segment": right},
            device_id_type=pl.DeviceIdType.MESH,
        )

    replica_k = pltpu.make_async_remote_copy(
        src_ref=stage_k, dst_ref=rk_ref, send_sem=rep_send.at[0], recv_sem=rep_recv.at[0],
        device_id={"segment": right}, device_id_type=pl.DeviceIdType.MESH,
    )
    replica_v = pltpu.make_async_remote_copy(
        src_ref=stage_v, dst_ref=rv_ref, send_sem=rep_send.at[1], recv_sem=rep_recv.at[1],
        device_id={"segment": right}, device_id_type=pl.DeviceIdType.MESH,
    )

    def fill(stage, pool):
        def one(r, carry):
            length = length_ref[r]
            last = jnp.maximum(length // PAGE - 1, 0)
            page = pool[table_ref[r, last]]
            finished = jnp.full(page.shape, lax.rem(length, PAGE), jnp.int32) == 0
            stage[r] = jnp.where(finished, page, jnp.zeros_like(page))
            return carry

        lax.fori_loop(0, rows, one, 0)

    def send_replicas():
        fill(stage_k, k_pool)
        replica_k.start()
        fill(stage_v, v_pool)
        replica_v.start()

    load_k.wait()
    load_v.wait()

    @pl.when(me != 0)
    def _():
        send_replicas()

    gain = gain_ref[...].astype(jnp.float32)
    pair = 2 * share
    top = lax.broadcasted_iota(jnp.int32, (pair, HEAD_DIM), 0) < share
    token = lax.broadcasted_iota(jnp.int32, (heads, context), 1)

    def attend(c, carry):
        pltpu.make_async_copy(x_in.at[rows_of(c)], x_in.at[rows_of(c)], recv_sem.at[c]).wait()
        x = x_in[rows_of(c)].astype(jnp.float32)
        mean_square = jnp.mean(x * x, axis=-1, keepdims=True)
        query = (x * lax.rsqrt(mean_square + EPSILON) * gain[None]).astype(jnp.bfloat16)
        fresh_k = nk_ref[rows_of(c)]
        fresh_v = nv_ref[rows_of(c)]

        def spread(fresh, i):
            return jnp.concatenate(
                [
                    jnp.broadcast_to(fresh[i : i + 1, g * HEAD_DIM : (g + 1) * HEAD_DIM], (share, HEAD_DIM))
                    for g in range(kv)
                ],
                axis=0,
            )

        scores = []
        ids = []
        for i in range(CHUNK):
            r = c * CHUNK + i
            ids.append([table_ref[r, p] for p in range(pages)])
            parts = []
            for g in range(kv // 2):
                cols = slice(g * 2 * HEAD_DIM, (g + 1) * 2 * HEAD_DIM)
                keys = jnp.concatenate([k_pool[j, :, cols] for j in ids[i]], axis=0)
                q = query[i, g * pair : (g + 1) * pair]
                zero = jnp.zeros_like(q)
                wide = jnp.concatenate(
                    [jnp.where(top, q, zero), jnp.where(top, zero, q)], axis=1
                )
                parts.append(
                    lax.dot_general(
                        wide, keys, (((1,), (1,)), ((), ())), preferred_element_type=jnp.float32
                    )
                )
            s = jnp.concatenate(parts, axis=0) * SCALE
            scores.append(jnp.where(token < length_ref[r], s, -1e30))
        scores = jnp.stack(scores)
        own = jnp.stack([spread(fresh_k, i) for i in range(CHUNK)])
        own = jnp.sum(query.astype(jnp.float32) * own, axis=-1, keepdims=True) * SCALE
        highest = jnp.maximum(jnp.max(scores, axis=-1, keepdims=True), own)
        weights = jnp.exp(scores - highest)
        own = jnp.exp(own - highest)
        share_of = 1.0 / (jnp.sum(weights, axis=-1, keepdims=True) + own)
        weights = (weights * share_of).astype(jnp.bfloat16)
        own = (own * share_of).astype(jnp.bfloat16).astype(jnp.float32)
        for i in range(CHUNK):
            parts = []
            for g in range(kv // 2):
                cols = slice(g * 2 * HEAD_DIM, (g + 1) * 2 * HEAD_DIM)
                values = jnp.concatenate([v_pool[j, :, cols] for j in ids[i]], axis=0)
                mixed = jnp.dot(
                    weights[i, g * pair : (g + 1) * pair], values, preferred_element_type=jnp.float32
                )
                parts += [mixed[:share, :HEAD_DIM], mixed[share:, HEAD_DIM:]]
            result = x[i] + jnp.concatenate(parts, axis=0) + own[i] * spread(fresh_v, i)
            out_ref[c * CHUNK + i] = result.astype(jnp.bfloat16)

        @pl.when(me < sections - 1)
        def _():
            send_of(c).start()

        return carry

    lax.fori_loop(0, chunks, attend, 0)

    @pl.when(me == 0)
    def _():
        send_replicas()

    @pl.when(me < sections - 1)
    def _():
        for c in range(chunks):
            send_of(c).wait_send()

    replica_k.wait()
    replica_v.wait()


def shards(sections, stream_in, cache_k, cache_v, new_k, new_v, q_gain, page_table, lengths):
    rows, width = stream_in.shape
    heads = width // HEAD_DIM
    pool = cache_k.shape[1:]
    anywhere = pl.BlockSpec(memory_space=pl.ANY)
    vmem = pl.BlockSpec(memory_space=pltpu.VMEM)
    smem = pl.BlockSpec(memory_space=pltpu.SMEM)
    kept = (rows,) + pool[1:]
    chunks = rows // CHUNK
    out, replica_k, replica_v = pl.pallas_call(
        functools.partial(relay_kernel, sections),
        out_shape=(
            jax.ShapeDtypeStruct((rows, heads, HEAD_DIM), jnp.bfloat16),
            jax.ShapeDtypeStruct(kept, jnp.bfloat16),
            jax.ShapeDtypeStruct(kept, jnp.bfloat16),
        ),
        in_specs=[anywhere, anywhere, anywhere, vmem, vmem, vmem, smem, smem],
        out_specs=(vmem, anywhere, anywhere),
        scratch_shapes=[
            pltpu.VMEM(pool, jnp.bfloat16),
            pltpu.VMEM(pool, jnp.bfloat16),
            pltpu.VMEM((rows, heads, HEAD_DIM), jnp.bfloat16),
            pltpu.VMEM(kept, jnp.bfloat16),
            pltpu.VMEM(kept, jnp.bfloat16),
            pltpu.SemaphoreType.DMA((2,)),
            pltpu.SemaphoreType.DMA((chunks,)),
            pltpu.SemaphoreType.DMA((chunks,)),
            pltpu.SemaphoreType.DMA((2,)),
            pltpu.SemaphoreType.DMA((2,)),
        ],
        compiler_params=pltpu.CompilerParams(
            collective_id=0, has_side_effects=True, vmem_limit_bytes=40 * 1024 * 1024
        ),
        name="relay",
    )(
        stream_in.reshape(rows, heads, HEAD_DIM),
        cache_k[0],
        cache_v[0],
        new_k[0].astype(jnp.float32),
        new_v[0].astype(jnp.float32),
        q_gain.reshape(heads, HEAD_DIM),
        page_table,
        lengths,
    )
    return (out.reshape(1, rows, width), replica_k[None], replica_v[None])


def solution(mesh):
    in_specs = (
        P("group", "tensor"),
        P("segment", "group", None, "tensor"),
        P("segment", "group", None, "tensor"),
        P("segment", "group", "tensor"),
        P("segment", "group", "tensor"),
        P("segment", "tensor"),
        P("group", None),
        P("group"),
    )
    out_specs = (
        P("segment", "group", "tensor"),
        P("segment", "group", None, "tensor"),
        P("segment", "group", None, "tensor"),
    )
    return jax.shard_map(
        functools.partial(shards, mesh.shape["segment"]),
        mesh=mesh, in_specs=in_specs, out_specs=out_specs, check_vma=False,
    )
```

```python
import functools

import jax
import jax.numpy as jnp
from jax import lax
from jax.experimental import pallas as pl
from jax.experimental.pallas import tpu as pltpu
from jax.sharding import PartitionSpec as P

HEAD_DIM = 128
PAGE = 16
EPSILON = 1e-06
SCALE = HEAD_DIM ** (-0.5)
CHUNK = 4
PIECE = 8
VMEM_BYTES = 60 * 1024 * 1024


def pieces_before(section):
    return section * 3 // 2


def relay_kernel(
    sections,
    x_hbm, k_hbm, v_hbm, nk_hbm, nv_hbm, gain_hbm, table_hbm, length_hbm,
    out_ref, replica_ref,
    k_pool, v_pool, x_raw, x_wide, x_in, stage, nk_ref, nv_ref, gain_row, gain_ref, table_ref, length_ref,
    load_sem, recv_sem, send_sem, rep_send, rep_recv,
):
    rows, heads, _ = x_in.shape
    kv = k_pool.shape[2] // HEAD_DIM
    share = heads // kv
    pages = table_ref.shape[0]
    context = pages * PAGE
    chunks = rows // CHUNK
    pieces = 2 * rows // PIECE
    me = lax.axis_index("segment")
    right = lax.rem(me + 1, sections)
    left = lax.rem(me + sections - 1, sections)

    loads = [
        pltpu.make_async_copy(source, target, load_sem.at[i])
        for i, (source, target) in enumerate(
            (
                (table_hbm, table_ref),
                (length_hbm, length_ref),
                (x_hbm, x_raw),
                (gain_hbm, gain_row),
                (nk_hbm, nk_ref),
                (nv_hbm, nv_ref),
                (k_hbm, k_pool),
                (v_hbm, v_pool),
            )
        )
    ]
    for load in loads:
        load.start()

    barrier = pltpu.get_barrier_semaphore()
    pl.semaphore_signal(
        barrier, inc=1, device_id={"segment": left}, device_id_type=pl.DeviceIdType.MESH
    )
    for load in loads[:4]:
        load.wait()

    def columns(h):
        return slice(h * HEAD_DIM, (h + 1) * HEAD_DIM)

    @pl.when(me == 0)
    def _():
        for h in range(heads):
            x_wide[:, h, :] = x_raw[:, columns(h)].astype(jnp.float32)
        x_in[...] = x_wide[...].astype(jnp.bfloat16)

    gain_wide = gain_row[...].astype(jnp.float32)
    for h in range(heads):
        gain_ref[h : h + 1, :] = gain_wide[:, columns(h)]

    for load in loads[4:]:
        load.wait()
    pl.semaphore_wait(barrier, 1)

    def rows_of(c):
        return pl.ds(c * CHUNK, CHUNK)

    def send_of(c):
        return pltpu.make_async_remote_copy(
            src_ref=out_ref.at[rows_of(c)],
            dst_ref=x_in.at[rows_of(c)],
            send_sem=send_sem.at[c],
            recv_sem=recv_sem.at[c],
            device_id={"segment": right},
            device_id_type=pl.DeviceIdType.MESH,
        )

    def piece_of(i):
        return pltpu.make_async_remote_copy(
            src_ref=stage.at[pl.ds(i * PIECE, PIECE)],
            dst_ref=replica_ref.at[pl.ds(i * PIECE, PIECE)],
            send_sem=rep_send.at[i],
            recv_sem=rep_recv.at[i],
            device_id={"segment": right},
            device_id_type=pl.DeviceIdType.MESH,
        )

    def fill():
        def one(r, carry):
            length = length_ref[r]
            last = jnp.maximum(length // PAGE - 1, 0)
            page_id = table_ref[last, r]
            for first, pool in ((0, k_pool), (rows, v_pool)):
                page = pool[page_id]
                finished = jnp.full(page.shape, lax.rem(length, PAGE), jnp.int32) == 0
                stage[first + r] = jnp.where(finished, page, jnp.zeros_like(page))
            return carry

        lax.fori_loop(0, rows, one, 0)

    def send_pieces(first, last):
        def one(i, carry):
            piece_of(i).start()
            return carry

        lax.fori_loop(first, last, one, 0)

    before = jnp.where(me == sections - 1, pieces, jnp.minimum(pieces_before(me), pieces))

    @pl.when(me != 0)
    def _():
        fill()
        send_pieces(0, before)

    gain = gain_ref[...]
    pair = 2 * share
    top = lax.broadcasted_iota(jnp.int32, (pair, HEAD_DIM), 0) < share
    token = lax.broadcasted_iota(jnp.int32, (heads, context), 1)

    def attend(c, fresh_k, fresh_v):
        @pl.when(me > 0)
        def _():
            send_of(c).wait_recv()

        x = x_in[rows_of(c)].astype(jnp.float32)
        mean_square = jnp.mean(x * x, axis=-1, keepdims=True)
        query = (x * lax.rsqrt(mean_square + EPSILON) * gain[None]).astype(jnp.bfloat16)

        def spread(fresh, i):
            return jnp.concatenate(
                [
                    jnp.broadcast_to(fresh[i : i + 1, columns(g)], (share, HEAD_DIM))
                    for g in range(kv)
                ],
                axis=0,
            )

        scores = []
        ids = []
        for i in range(CHUNK):
            r = c * CHUNK + i
            ids.append([table_ref[p, r] for p in range(pages)])
            parts = []
            for g in range(kv // 2):
                cols = slice(g * 2 * HEAD_DIM, (g + 1) * 2 * HEAD_DIM)
                keys = jnp.concatenate([k_pool[j, :, cols] for j in ids[i]], axis=0)
                q = query[i, g * pair : (g + 1) * pair]
                zero = jnp.zeros_like(q)
                wide = jnp.concatenate(
                    [jnp.where(top, q, zero), jnp.where(top, zero, q)], axis=1
                )
                parts.append(
                    lax.dot_general(
                        wide, keys, (((1,), (1,)), ((), ())), preferred_element_type=jnp.float32
                    )
                )
            s = jnp.concatenate(parts, axis=0) * SCALE
            scores.append(jnp.where(token < length_ref[r], s, -1e30))
        scores = jnp.stack(scores)
        own = jnp.stack([spread(fresh_k, i) for i in range(CHUNK)])
        own = jnp.sum(query.astype(jnp.float32) * own, axis=-1, keepdims=True) * SCALE
        highest = jnp.maximum(jnp.max(scores, axis=-1, keepdims=True), own)
        weights = jnp.exp(scores - highest)
        own = jnp.exp(own - highest)
        share_of = 1.0 / (jnp.sum(weights, axis=-1, keepdims=True) + own)
        weights = (weights * share_of).astype(jnp.bfloat16)
        own = (own * share_of).astype(jnp.bfloat16).astype(jnp.float32)
        for i in range(CHUNK):
            parts = []
            for g in range(kv // 2):
                cols = slice(g * 2 * HEAD_DIM, (g + 1) * 2 * HEAD_DIM)
                values = jnp.concatenate([v_pool[j, :, cols] for j in ids[i]], axis=0)
                mixed = jnp.dot(
                    weights[i, g * pair : (g + 1) * pair], values, preferred_element_type=jnp.float32
                )
                parts += [mixed[:share, :HEAD_DIM], mixed[share:, HEAD_DIM:]]
            result = x[i] + jnp.concatenate(parts, axis=0) + own[i] * spread(fresh_v, i)
            out_ref[c * CHUNK + i] = result.astype(jnp.bfloat16)

        @pl.when(me < sections - 1)
        def _():
            send_of(c).start()

    block = max(CHUNK, 16)

    def attend_block(b, carry):
        at = pl.ds(pl.multiple_of(b * block, block), block)
        fresh_k = nk_ref[at, :].astype(jnp.float32)
        fresh_v = nv_ref[at, :].astype(jnp.float32)
        for j in range(block // CHUNK):
            own = slice(j * CHUNK, (j + 1) * CHUNK)
            attend(b * (block // CHUNK) + j, fresh_k[own], fresh_v[own])
        return carry

    lax.fori_loop(0, rows // block, attend_block, 0)

    @pl.when(me == 0)
    def _():
        fill()
        send_pieces(0, before)

    send_pieces(before, pieces)

    @pl.when(me < sections - 1)
    def _():
        for c in range(chunks):
            send_of(c).wait_send()

    for i in range(pieces):
        piece_of(i).wait()


def shards(sections, stream_in, cache_k, cache_v, new_k, new_v, q_gain, page_table, lengths):
    rows, width = stream_in.shape
    heads = width // HEAD_DIM
    pool = cache_k.shape[1:]
    hbm = pl.BlockSpec(memory_space=pltpu.HBM)
    vmem = pl.BlockSpec(memory_space=pltpu.VMEM)
    chunks = rows // CHUNK
    pieces = 2 * rows // PIECE
    fresh = new_k.shape[1:]
    both = (2 * rows,) + pool[1:]
    out, replicas = pl.pallas_call(
        functools.partial(relay_kernel, sections),
        out_shape=(
            jax.ShapeDtypeStruct((rows, heads, HEAD_DIM), jnp.bfloat16),
            jax.ShapeDtypeStruct(both, jnp.bfloat16),
        ),
        in_specs=[hbm] * 8,
        out_specs=(vmem, vmem),
        scratch_shapes=[
            pltpu.VMEM(pool, jnp.bfloat16),
            pltpu.VMEM(pool, jnp.bfloat16),
            pltpu.VMEM((rows, width), jnp.bfloat16),
            pltpu.VMEM((rows, heads, HEAD_DIM), jnp.float32),
            pltpu.VMEM((rows, heads, HEAD_DIM), jnp.bfloat16),
            pltpu.VMEM(both, jnp.bfloat16),
            pltpu.VMEM(fresh, jnp.bfloat16),
            pltpu.VMEM(fresh, jnp.bfloat16),
            pltpu.VMEM((1, width), jnp.bfloat16),
            pltpu.VMEM((heads, HEAD_DIM), jnp.float32),
            pltpu.SMEM(page_table.shape[::-1], jnp.int32),
            pltpu.SMEM(lengths.shape, jnp.int32),
            pltpu.SemaphoreType.DMA((8,)),
            pltpu.SemaphoreType.DMA((chunks,)),
            pltpu.SemaphoreType.DMA((chunks,)),
            pltpu.SemaphoreType.DMA((pieces,)),
            pltpu.SemaphoreType.DMA((pieces,)),
        ],
        compiler_params=pltpu.CompilerParams(
            collective_id=0, has_side_effects=True, vmem_limit_bytes=VMEM_BYTES
        ),
        name="relay",
    )(
        stream_in,
        cache_k[0],
        cache_v[0],
        new_k[0],
        new_v[0],
        q_gain,
        page_table.T,
        lengths,
    )
    return (out.reshape(1, rows, width), replicas[None, :rows], replicas[None, rows:])


def solution(mesh):
    in_specs = (
        P("group", "tensor"),
        P("segment", "group", None, "tensor"),
        P("segment", "group", None, "tensor"),
        P("segment", "group", "tensor"),
        P("segment", "group", "tensor"),
        P("segment", "tensor"),
        P("group", None),
        P("group"),
    )
    out_specs = (
        P("segment", "group", "tensor"),
        P("segment", "group", None, "tensor"),
        P("segment", "group", None, "tensor"),
    )
    return jax.shard_map(
        functools.partial(shards, mesh.shape["segment"]),
        mesh=mesh, in_specs=in_specs, out_specs=out_specs, check_vma=False,
    )
```

```python
import functools

import jax
import jax.numpy as jnp
from jax import lax
from jax.experimental import pallas as pl
from jax.experimental.pallas import tpu as pltpu
from jax.sharding import PartitionSpec as P

HEAD_DIM = 128
PAGE = 16
EPSILON = 1e-06
SCALE = HEAD_DIM ** (-0.5)
CHUNK = 4
PIECE = 8
VMEM_BYTES = 60 * 1024 * 1024


def pieces_before(section):
    return section * 5 // 4


def relay_kernel(
    sections,
    x_hbm, k_hbm, v_hbm, nk_hbm, nv_hbm, gain_hbm, table_hbm, length_hbm,
    out_ref, replica_ref,
    k_pool, v_pool, x_raw, x_wide, x_in, stage, nk_ref, nv_ref, gain_row, gain_ref, table_ref, length_ref,
    load_sem, recv_sem, send_sem, rep_send, rep_recv,
):
    rows, heads, _ = x_in.shape
    kv = k_pool.shape[2] // HEAD_DIM
    share = heads // kv
    pages = table_ref.shape[0]
    context = pages * PAGE
    chunks = rows // CHUNK
    pieces = 2 * rows // PIECE
    me = lax.axis_index("segment")
    right = lax.rem(me + 1, sections)
    left = lax.rem(me + sections - 1, sections)

    loads = [
        pltpu.make_async_copy(source, target, load_sem.at[i])
        for i, (source, target) in enumerate(
            (
                (table_hbm, table_ref),
                (length_hbm, length_ref),
                (x_hbm, x_raw),
                (gain_hbm, gain_row),
                (nk_hbm, nk_ref),
                (nv_hbm, nv_ref),
                (k_hbm, k_pool),
                (v_hbm, v_pool),
            )
        )
    ]
    for load in loads:
        load.start()

    barrier = pltpu.get_barrier_semaphore()
    pl.semaphore_signal(
        barrier, inc=1, device_id={"segment": left}, device_id_type=pl.DeviceIdType.MESH
    )
    for load in loads[:4]:
        load.wait()

    def columns(h):
        return slice(h * HEAD_DIM, (h + 1) * HEAD_DIM)

    @pl.when(me == 0)
    def _():
        for h in range(heads):
            x_wide[:, h, :] = x_raw[:, columns(h)].astype(jnp.float32)
        x_in[...] = x_wide[...].astype(jnp.bfloat16)

    gain_wide = gain_row[...].astype(jnp.float32)
    for h in range(heads):
        gain_ref[h : h + 1, :] = gain_wide[:, columns(h)]

    for load in loads[4:]:
        load.wait()
    pl.semaphore_wait(barrier, 1)

    def rows_of(c):
        return pl.ds(c * CHUNK, CHUNK)

    def send_of(c):
        return pltpu.make_async_remote_copy(
            src_ref=out_ref.at[rows_of(c)],
            dst_ref=x_in.at[rows_of(c)],
            send_sem=send_sem.at[c],
            recv_sem=recv_sem.at[c],
            device_id={"segment": right},
            device_id_type=pl.DeviceIdType.MESH,
        )

    def piece_of(i):
        return pltpu.make_async_remote_copy(
            src_ref=stage.at[pl.ds(i * PIECE, PIECE)],
            dst_ref=replica_ref.at[pl.ds(i * PIECE, PIECE)],
            send_sem=rep_send.at[i],
            recv_sem=rep_recv.at[i],
            device_id={"segment": right},
            device_id_type=pl.DeviceIdType.MESH,
        )

    def fill():
        def one(r, carry):
            length = length_ref[r]
            last = jnp.maximum(length // PAGE - 1, 0)
            page_id = table_ref[last, r]
            for first, pool in ((0, k_pool), (rows, v_pool)):
                page = pool[page_id]
                finished = jnp.full(page.shape, lax.rem(length, PAGE), jnp.int32) == 0
                stage[first + r] = jnp.where(finished, page, jnp.zeros_like(page))
            return carry

        lax.fori_loop(0, rows, one, 0)

    def send_pieces(first, last):
        def one(i, carry):
            piece_of(i).start()
            return carry

        lax.fori_loop(first, last, one, 0)

    before = jnp.where(me == sections - 1, pieces, jnp.minimum(pieces_before(me), pieces))

    @pl.when(me != 0)
    def _():
        fill()
        send_pieces(0, before)

    gain = gain_ref[...]
    pair = 2 * share
    top = lax.broadcasted_iota(jnp.int32, (pair, HEAD_DIM), 0) < share
    token = lax.broadcasted_iota(jnp.int32, (heads, context), 1)

    def attend(c, fresh_k, fresh_v):
        @pl.when(me > 0)
        def _():
            send_of(c).wait_recv()

        x = x_in[rows_of(c)].astype(jnp.float32)
        mean_square = jnp.mean(x * x, axis=-1, keepdims=True)
        query = (x * lax.rsqrt(mean_square + EPSILON) * gain[None]).astype(jnp.bfloat16)

        def spread(fresh, i):
            return jnp.concatenate(
                [
                    jnp.broadcast_to(fresh[i : i + 1, columns(g)], (share, HEAD_DIM))
                    for g in range(kv)
                ],
                axis=0,
            )

        scores = []
        ids = []
        for i in range(CHUNK):
            r = c * CHUNK + i
            ids.append([table_ref[p, r] for p in range(pages)])
            parts = []
            for g in range(kv // 2):
                cols = slice(g * 2 * HEAD_DIM, (g + 1) * 2 * HEAD_DIM)
                keys = jnp.concatenate([k_pool[j, :, cols] for j in ids[i]], axis=0)
                q = query[i, g * pair : (g + 1) * pair]
                zero = jnp.zeros_like(q)
                wide = jnp.concatenate(
                    [jnp.where(top, q, zero), jnp.where(top, zero, q)], axis=1
                )
                parts.append(
                    lax.dot_general(
                        wide, keys, (((1,), (1,)), ((), ())), preferred_element_type=jnp.float32
                    )
                )
            s = jnp.concatenate(parts, axis=0) * SCALE
            scores.append(jnp.where(token < length_ref[r], s, -1e30))
        scores = jnp.stack(scores)
        own = jnp.stack([spread(fresh_k, i) for i in range(CHUNK)])
        own = jnp.sum(query.astype(jnp.float32) * own, axis=-1, keepdims=True) * SCALE
        highest = jnp.maximum(jnp.max(scores, axis=-1, keepdims=True), own)
        weights = jnp.exp(scores - highest)
        own = jnp.exp(own - highest)
        share_of = 1.0 / (jnp.sum(weights, axis=-1, keepdims=True) + own)
        weights = (weights * share_of).astype(jnp.bfloat16)
        own = (own * share_of).astype(jnp.bfloat16).astype(jnp.float32)
        for i in range(CHUNK):
            parts = []
            for g in range(kv // 2):
                cols = slice(g * 2 * HEAD_DIM, (g + 1) * 2 * HEAD_DIM)
                values = jnp.concatenate([v_pool[j, :, cols] for j in ids[i]], axis=0)
                mixed = jnp.dot(
                    weights[i, g * pair : (g + 1) * pair], values, preferred_element_type=jnp.float32
                )
                parts += [mixed[:share, :HEAD_DIM], mixed[share:, HEAD_DIM:]]
            result = x[i] + jnp.concatenate(parts, axis=0) + own[i] * spread(fresh_v, i)
            out_ref[c * CHUNK + i] = result.astype(jnp.bfloat16)

        @pl.when(me < sections - 1)
        def _():
            send_of(c).start()

    block = max(CHUNK, 16)

    def attend_block(b, carry):
        at = pl.ds(pl.multiple_of(b * block, block), block)
        fresh_k = nk_ref[at, :].astype(jnp.float32)
        fresh_v = nv_ref[at, :].astype(jnp.float32)
        for j in range(block // CHUNK):
            own = slice(j * CHUNK, (j + 1) * CHUNK)
            attend(b * (block // CHUNK) + j, fresh_k[own], fresh_v[own])
        return carry

    lax.fori_loop(0, rows // block, attend_block, 0)

    @pl.when(me == 0)
    def _():
        fill()
        send_pieces(0, before)

    send_pieces(before, pieces)

    @pl.when(me < sections - 1)
    def _():
        for c in range(chunks):
            send_of(c).wait_send()

    for i in range(pieces):
        piece_of(i).wait()


def finish_kernel(x_hbm, pages_hbm, out_hbm, rk_hbm, rv_hbm, x, wide, flat, pages, sem):
    rows, heads, _ = x.shape
    load_x = pltpu.make_async_copy(x_hbm, x, sem.at[0])
    load_x.start()
    halves = [pl.ds(0, rows), pl.ds(rows, rows)]
    load_pages = [
        pltpu.make_async_copy(pages_hbm.at[half], pages.at[half], sem.at[1 + i])
        for i, half in enumerate(halves)
    ]
    for load in load_pages:
        load.start()
    load_x.wait()
    wide[...] = x[...].astype(jnp.float32)
    for h in range(heads):
        flat[:, h * HEAD_DIM : (h + 1) * HEAD_DIM] = wide[:, h, :].astype(jnp.bfloat16)
    stores = [pltpu.make_async_copy(flat, out_hbm.at[0], sem.at[3])]
    stores[0].start()
    for i, target in enumerate((rk_hbm, rv_hbm)):
        load_pages[i].wait()
        store = pltpu.make_async_copy(pages.at[halves[i]], target.at[0], sem.at[4 + i])
        store.start()
        stores.append(store)
    for store in stores:
        store.wait()


def shards(sections, stream_in, cache_k, cache_v, new_k, new_v, q_gain, page_table, lengths):
    rows, width = stream_in.shape
    heads = width // HEAD_DIM
    pool = cache_k.shape[1:]
    hbm = pl.BlockSpec(memory_space=pltpu.HBM)
    vmem = pl.BlockSpec(memory_space=pltpu.VMEM)
    chunks = rows // CHUNK
    pieces = 2 * rows // PIECE
    fresh = new_k.shape[1:]
    both = (2 * rows,) + pool[1:]
    out, replicas = pl.pallas_call(
        functools.partial(relay_kernel, sections),
        out_shape=(
            jax.ShapeDtypeStruct((rows, heads, HEAD_DIM), jnp.bfloat16),
            jax.ShapeDtypeStruct(both, jnp.bfloat16),
        ),
        in_specs=[hbm] * 8,
        out_specs=(vmem, vmem),
        scratch_shapes=[
            pltpu.VMEM(pool, jnp.bfloat16),
            pltpu.VMEM(pool, jnp.bfloat16),
            pltpu.VMEM((rows, width), jnp.bfloat16),
            pltpu.VMEM((rows, heads, HEAD_DIM), jnp.float32),
            pltpu.VMEM((rows, heads, HEAD_DIM), jnp.bfloat16),
            pltpu.VMEM(both, jnp.bfloat16),
            pltpu.VMEM(fresh, jnp.bfloat16),
            pltpu.VMEM(fresh, jnp.bfloat16),
            pltpu.VMEM((1, width), jnp.bfloat16),
            pltpu.VMEM((heads, HEAD_DIM), jnp.float32),
            pltpu.SMEM(page_table.shape[::-1], jnp.int32),
            pltpu.SMEM(lengths.shape, jnp.int32),
            pltpu.SemaphoreType.DMA((8,)),
            pltpu.SemaphoreType.DMA((chunks,)),
            pltpu.SemaphoreType.DMA((chunks,)),
            pltpu.SemaphoreType.DMA((pieces,)),
            pltpu.SemaphoreType.DMA((pieces,)),
        ],
        compiler_params=pltpu.CompilerParams(
            collective_id=0, has_side_effects=True, vmem_limit_bytes=VMEM_BYTES
        ),
        name="relay",
    )(
        stream_in,
        cache_k[0],
        cache_v[0],
        new_k[0],
        new_v[0],
        q_gain,
        page_table.T,
        lengths,
    )
    kept = (1, rows) + pool[1:]
    return pl.pallas_call(
        finish_kernel,
        out_shape=(
            jax.ShapeDtypeStruct((1, rows, width), jnp.bfloat16),
            jax.ShapeDtypeStruct(kept, jnp.bfloat16),
            jax.ShapeDtypeStruct(kept, jnp.bfloat16),
        ),
        in_specs=[hbm, hbm],
        out_specs=(hbm, hbm, hbm),
        scratch_shapes=[
            pltpu.VMEM((rows, heads, HEAD_DIM), jnp.bfloat16),
            pltpu.VMEM((rows, heads, HEAD_DIM), jnp.float32),
            pltpu.VMEM((rows, width), jnp.bfloat16),
            pltpu.VMEM(both, jnp.bfloat16),
            pltpu.SemaphoreType.DMA((6,)),
        ],
        compiler_params=pltpu.CompilerParams(vmem_limit_bytes=VMEM_BYTES),
        name="finish",
    )(out, replicas)


def solution(mesh):
    in_specs = (
        P("group", "tensor"),
        P("segment", "group", None, "tensor"),
        P("segment", "group", None, "tensor"),
        P("segment", "group", "tensor"),
        P("segment", "group", "tensor"),
        P("segment", "tensor"),
        P("group", None),
        P("group"),
    )
    out_specs = (
        P("segment", "group", "tensor"),
        P("segment", "group", None, "tensor"),
        P("segment", "group", None, "tensor"),
    )
    return jax.shard_map(
        functools.partial(shards, mesh.shape["segment"]),
        mesh=mesh, in_specs=in_specs, out_specs=out_specs, check_vma=False,
    )
```

```python
import functools

import jax
import jax.numpy as jnp
from jax import lax
from jax.experimental import pallas as pl
from jax.experimental.pallas import tpu as pltpu
from jax.sharding import PartitionSpec as P

HEAD_DIM = 128
PAGE = 16
EPSILON = 1e-06
SCALE = HEAD_DIM ** (-0.5)
CHUNK = 4
PIECE = 8
VMEM_BYTES = 60 * 1024 * 1024


def pieces_before(section):
    return section * 3 // 2


def relay_kernel(
    sections,
    x_hbm, k_hbm, v_hbm, nk_hbm, nv_hbm, gain_hbm, table_hbm, length_hbm,
    out_ref, replica_ref,
    k_pool, v_pool, x_raw, x_wide, x_in, stage, nk_ref, nv_ref, gain_row, gain_ref, table_ref, length_ref,
    load_sem, recv_sem, send_sem, rep_send, rep_recv,
):
    rows, heads, _ = x_in.shape
    kv = k_pool.shape[2] // HEAD_DIM
    share = heads // kv
    pages = table_ref.shape[0]
    context = pages * PAGE
    chunks = rows // CHUNK
    pieces = 2 * rows // PIECE
    me = lax.axis_index("segment")
    right = lax.rem(me + 1, sections)
    left = lax.rem(me + sections - 1, sections)

    loads = [
        pltpu.make_async_copy(source, target, load_sem.at[i])
        for i, (source, target) in enumerate(
            (
                (table_hbm, table_ref),
                (length_hbm, length_ref),
                (x_hbm, x_raw),
                (gain_hbm, gain_row),
                (nk_hbm, nk_ref),
                (nv_hbm, nv_ref),
                (k_hbm, k_pool),
                (v_hbm, v_pool),
            )
        )
    ]
    for load in loads:
        load.start()

    barrier = pltpu.get_barrier_semaphore()
    pl.semaphore_signal(
        barrier, inc=1, device_id={"segment": left}, device_id_type=pl.DeviceIdType.MESH
    )
    for load in loads[:4]:
        load.wait()

    def columns(h):
        return slice(h * HEAD_DIM, (h + 1) * HEAD_DIM)

    @pl.when(me == 0)
    def _():
        for h in range(heads):
            x_wide[:, h, :] = x_raw[:, columns(h)].astype(jnp.float32)
        x_in[...] = x_wide[...].astype(jnp.bfloat16)

    gain_wide = gain_row[...].astype(jnp.float32)
    for h in range(heads):
        gain_ref[h : h + 1, :] = gain_wide[:, columns(h)]

    for load in loads[4:7]:
        load.wait()
    pl.semaphore_wait(barrier, 1)

    def rows_of(c):
        return pl.ds(c * CHUNK, CHUNK)

    def send_of(c):
        return pltpu.make_async_remote_copy(
            src_ref=out_ref.at[rows_of(c)],
            dst_ref=x_in.at[rows_of(c)],
            send_sem=send_sem.at[c],
            recv_sem=recv_sem.at[c],
            device_id={"segment": right},
            device_id_type=pl.DeviceIdType.MESH,
        )

    def piece_of(i):
        return pltpu.make_async_remote_copy(
            src_ref=stage.at[pl.ds(i * PIECE, PIECE)],
            dst_ref=replica_ref.at[pl.ds(i * PIECE, PIECE)],
            send_sem=rep_send.at[i],
            recv_sem=rep_recv.at[i],
            device_id={"segment": right},
            device_id_type=pl.DeviceIdType.MESH,
        )

    def fill(first, pool):
        def one(b, carry):
            for j in range(4):
                r = b * 4 + j
                length = length_ref[r]
                last = jnp.maximum(length // PAGE - 1, 0)
                page = pool[table_ref[last, r]]
                finished = jnp.full(page.shape, lax.rem(length, PAGE), jnp.int32) == 0
                stage[first + r] = jnp.where(finished, page, jnp.zeros_like(page))
            return carry

        lax.fori_loop(0, rows // 4, one, 0)

    def send_pieces(first, last):
        def one(i, carry):
            piece_of(i).start()
            return carry

        lax.fori_loop(first, last, one, 0)

    before = jnp.where(me == sections - 1, pieces, jnp.minimum(pieces_before(me), pieces))

    half = pieces // 2

    @pl.when(me != 0)
    def _():
        fill(0, k_pool)
        send_pieces(0, jnp.minimum(before, half))

    loads[7].wait()

    @pl.when(me != 0)
    def _():
        fill(rows, v_pool)
        send_pieces(jnp.minimum(before, half), before)

    gain = gain_ref[...]
    pair = 2 * share
    top = lax.broadcasted_iota(jnp.int32, (pair, HEAD_DIM), 0) < share
    token = lax.broadcasted_iota(jnp.int32, (heads, context), 1)

    def attend(c, fresh_k, fresh_v):
        @pl.when(me > 0)
        def _():
            send_of(c).wait_recv()

        x = x_in[rows_of(c)].astype(jnp.float32)
        mean_square = jnp.mean(x * x, axis=-1, keepdims=True)
        query = (x * lax.rsqrt(mean_square + EPSILON) * gain[None]).astype(jnp.bfloat16)

        def spread(fresh, i):
            return jnp.concatenate(
                [
                    jnp.broadcast_to(fresh[i : i + 1, columns(g)], (share, HEAD_DIM))
                    for g in range(kv)
                ],
                axis=0,
            )

        scores = []
        ids = []
        for i in range(CHUNK):
            r = c * CHUNK + i
            ids.append([table_ref[p, r] for p in range(pages)])
            parts = []
            for g in range(kv // 2):
                cols = slice(g * 2 * HEAD_DIM, (g + 1) * 2 * HEAD_DIM)
                keys = jnp.concatenate([k_pool[j, :, cols] for j in ids[i]], axis=0)
                q = query[i, g * pair : (g + 1) * pair]
                zero = jnp.zeros_like(q)
                wide = jnp.concatenate(
                    [jnp.where(top, q, zero), jnp.where(top, zero, q)], axis=1
                )
                parts.append(
                    lax.dot_general(
                        wide, keys, (((1,), (1,)), ((), ())), preferred_element_type=jnp.float32
                    )
                )
            s = jnp.concatenate(parts, axis=0)
            scores.append(jnp.where(token < length_ref[r], s, -1e30))
        scores = jnp.stack(scores)
        own = jnp.stack([spread(fresh_k, i) for i in range(CHUNK)])
        own = jnp.sum(query.astype(jnp.float32) * own, axis=-1, keepdims=True)
        highest = jnp.maximum(jnp.max(scores, axis=-1, keepdims=True), own)
        weights = jnp.exp((scores - highest) * SCALE)
        own = jnp.exp((own - highest) * SCALE)
        share_of = 1.0 / (jnp.sum(weights, axis=-1, keepdims=True) + own)
        weights = weights.astype(jnp.bfloat16)
        own = own.astype(jnp.bfloat16).astype(jnp.float32)
        for i in range(CHUNK):
            parts = []
            for g in range(kv // 2):
                cols = slice(g * 2 * HEAD_DIM, (g + 1) * 2 * HEAD_DIM)
                values = jnp.concatenate([v_pool[j, :, cols] for j in ids[i]], axis=0)
                mixed = jnp.dot(
                    weights[i, g * pair : (g + 1) * pair], values, preferred_element_type=jnp.float32
                )
                parts += [mixed[:share, :HEAD_DIM], mixed[share:, HEAD_DIM:]]
            result = x[i] + (jnp.concatenate(parts, axis=0) + own[i] * spread(fresh_v, i)) * share_of[i]
            out_ref[c * CHUNK + i] = result.astype(jnp.bfloat16)

        @pl.when(me < sections - 1)
        def _():
            send_of(c).start()

    block = max(CHUNK, 16)

    def attend_block(b, carry):
        at = pl.ds(pl.multiple_of(b * block, block), block)
        fresh_k = nk_ref[at, :].astype(jnp.float32)
        fresh_v = nv_ref[at, :].astype(jnp.float32)
        for j in range(block // CHUNK):
            own = slice(j * CHUNK, (j + 1) * CHUNK)
            attend(b * (block // CHUNK) + j, fresh_k[own], fresh_v[own])
        return carry

    lax.fori_loop(0, rows // block, attend_block, 0)

    @pl.when(me == 0)
    def _():
        fill(0, k_pool)
        fill(rows, v_pool)
        send_pieces(0, before)

    send_pieces(before, pieces)

    @pl.when(me < sections - 1)
    def _():
        for c in range(chunks):
            send_of(c).wait_send()

    for i in range(pieces):
        piece_of(i).wait()


def finish_kernel(x_hbm, pages_hbm, out_hbm, rk_hbm, rv_hbm, x, wide, flat, pages, sem):
    rows, heads, _ = x.shape
    load_x = pltpu.make_async_copy(x_hbm, x, sem.at[0])
    load_x.start()
    halves = [pl.ds(0, rows), pl.ds(rows, rows)]
    load_pages = [
        pltpu.make_async_copy(pages_hbm.at[half], pages.at[half], sem.at[1 + i])
        for i, half in enumerate(halves)
    ]
    for load in load_pages:
        load.start()
    load_x.wait()
    wide[...] = x[...].astype(jnp.float32)
    for h in range(heads):
        flat[:, h * HEAD_DIM : (h + 1) * HEAD_DIM] = wide[:, h, :].astype(jnp.bfloat16)
    stores = [pltpu.make_async_copy(flat, out_hbm.at[0], sem.at[3])]
    stores[0].start()
    for i, target in enumerate((rk_hbm, rv_hbm)):
        load_pages[i].wait()
        store = pltpu.make_async_copy(pages.at[halves[i]], target.at[0], sem.at[4 + i])
        store.start()
        stores.append(store)
    for store in stores:
        store.wait()


def shards(sections, stream_in, cache_k, cache_v, new_k, new_v, q_gain, page_table, lengths):
    rows, width = stream_in.shape
    heads = width // HEAD_DIM
    pool = cache_k.shape[1:]
    hbm = pl.BlockSpec(memory_space=pltpu.HBM)
    vmem = pl.BlockSpec(memory_space=pltpu.VMEM)
    chunks = rows // CHUNK
    pieces = 2 * rows // PIECE
    fresh = new_k.shape[1:]
    both = (2 * rows,) + pool[1:]
    out, replicas = pl.pallas_call(
        functools.partial(relay_kernel, sections),
        out_shape=(
            jax.ShapeDtypeStruct((rows, heads, HEAD_DIM), jnp.bfloat16),
            jax.ShapeDtypeStruct(both, jnp.bfloat16),
        ),
        in_specs=[hbm] * 8,
        out_specs=(vmem, vmem),
        scratch_shapes=[
            pltpu.VMEM(pool, jnp.bfloat16),
            pltpu.VMEM(pool, jnp.bfloat16),
            pltpu.VMEM((rows, width), jnp.bfloat16),
            pltpu.VMEM((rows, heads, HEAD_DIM), jnp.float32),
            pltpu.VMEM((rows, heads, HEAD_DIM), jnp.bfloat16),
            pltpu.VMEM(both, jnp.bfloat16),
            pltpu.VMEM(fresh, jnp.bfloat16),
            pltpu.VMEM(fresh, jnp.bfloat16),
            pltpu.VMEM((1, width), jnp.bfloat16),
            pltpu.VMEM((heads, HEAD_DIM), jnp.float32),
            pltpu.SMEM(page_table.shape[::-1], jnp.int32),
            pltpu.SMEM(lengths.shape, jnp.int32),
            pltpu.SemaphoreType.DMA((8,)),
            pltpu.SemaphoreType.DMA((chunks,)),
            pltpu.SemaphoreType.DMA((chunks,)),
            pltpu.SemaphoreType.DMA((pieces,)),
            pltpu.SemaphoreType.DMA((pieces,)),
        ],
        compiler_params=pltpu.CompilerParams(
            collective_id=0, has_side_effects=True, vmem_limit_bytes=VMEM_BYTES
        ),
        name="relay",
    )(
        stream_in,
        cache_k[0],
        cache_v[0],
        new_k[0],
        new_v[0],
        q_gain,
        page_table.T,
        lengths,
    )
    kept = (1, rows) + pool[1:]
    return pl.pallas_call(
        finish_kernel,
        out_shape=(
            jax.ShapeDtypeStruct((1, rows, width), jnp.bfloat16),
            jax.ShapeDtypeStruct(kept, jnp.bfloat16),
            jax.ShapeDtypeStruct(kept, jnp.bfloat16),
        ),
        in_specs=[hbm, hbm],
        out_specs=(hbm, hbm, hbm),
        scratch_shapes=[
            pltpu.VMEM((rows, heads, HEAD_DIM), jnp.bfloat16),
            pltpu.VMEM((rows, heads, HEAD_DIM), jnp.float32),
            pltpu.VMEM((rows, width), jnp.bfloat16),
            pltpu.VMEM(both, jnp.bfloat16),
            pltpu.SemaphoreType.DMA((6,)),
        ],
        compiler_params=pltpu.CompilerParams(vmem_limit_bytes=VMEM_BYTES),
        name="finish",
    )(out, replicas)


def solution(mesh):
    in_specs = (
        P("group", "tensor"),
        P("segment", "group", None, "tensor"),
        P("segment", "group", None, "tensor"),
        P("segment", "group", "tensor"),
        P("segment", "group", "tensor"),
        P("segment", "tensor"),
        P("group", None),
        P("group"),
    )
    out_specs = (
        P("segment", "group", "tensor"),
        P("segment", "group", None, "tensor"),
        P("segment", "group", None, "tensor"),
    )
    return jax.shard_map(
        functools.partial(shards, mesh.shape["segment"]),
        mesh=mesh, in_specs=in_specs, out_specs=out_specs, check_vma=False,
    )
```
